32 devices in a mesh: groups: 2 (over y), clus: 4 (over z), sub: 2 (over x), rep: 2 (over core).
Axes of the slice: x: 2, y: 2, z: 4, core: 2. Of those that a mesh axis runs over, the one named last changes fastest.
Arguments:
- embeddings: bfloat16 [128, 256, 1024], P(('groups', 'clus', 'sub')), parts along dimension 0, may hold values from -2000 to 2000
- counts: int32 [128], P('groups'), parts along dimension 0, may hold values from 64 to 256
- partner: int32 [2, 32, 4], P(None, ('groups', 'clus', 'sub', 'rep')), parts along dimension 1, may hold values from -1 to 63, as said below
Outputs:
- log_density: float32 [128, 256], P(('groups', 'clus', 'sub')), parts along dimension 0
The draws below stay inside these ranges and needn't reach their ends.
There are 2 independent parts, one for each index of `groups`. The reference program is written for one: setup_inputs(seed, part) draws one part's arguments, and reference() takes and returns one part's arrays. A program takes and returns all parts, laid end to end along the dimension named above; each array names one. Nothing has to cross between parts.
Inputs may be any that keep to these rules, and one draw needn't show every extreme that they name: `partner`: slot d = (2 c + s) * 2 + r names only blocks of the clusters p * 2 + s with p != c, entry p naming a block of cluster p * 2 + s, so at most one block of each clus index in a batch; the number of named blocks differs from slot to slot, and in each batch some slot names one on every other clus index.
All inputs are finite; a program needn't handle non-finite values.
Results may differ from the reference program's by a relative error of at most 0.00045.
Values may be sent and summed in bfloat16 or wider, within the bound.
A program may use at most 128 MiB of HBM per device.

```python
import jax
import jax.numpy as jnp
from jax import lax

D = 1024
BLK = 256
BPD = 8
BATCHES = 2
NBLK = 64
N_CLUS = 4
N_SUB = 2
N_REP = 2


def draw_partner(key, part):
    devices_part = N_CLUS * N_SUB * N_REP
    key_count, key_order, key_pick, key_full = jax.random.split(key, 4)
    raw_counts = jax.random.randint(key_count, (BATCHES, devices_part), 0, N_CLUS)
    live_count = jnp.minimum(1 + raw_counts * raw_counts // max(N_CLUS - 1, 1), N_CLUS - 1)
    busiest = jax.random.randint(key_full, (BATCHES, 1), 0, devices_part)
    device_ids = jnp.arange(devices_part, dtype=jnp.int32)
    live_count = jnp.where(device_ids[None, :] == busiest, N_CLUS - 1, live_count)
    own_clus = device_ids // (N_SUB * N_REP)
    own_sub = device_ids // N_REP % N_SUB
    peer_ids = jnp.arange(N_CLUS, dtype=jnp.int32)
    scores = jax.random.randint(key_order, (BATCHES, devices_part, N_CLUS), 0, 1 << 20) * N_CLUS + peer_ids
    scores = jnp.where(peer_ids[None, None, :] == own_clus[None, :, None], 1 << 30, scores)
    peer_rank = jnp.sum((scores[..., None, :] < scores[..., :, None]).astype(jnp.int32), axis=-1)
    is_live = peer_rank < live_count[:, :, None]
    picked = jax.random.randint(key_pick, (BATCHES, devices_part, N_CLUS), 0, BPD)
    targets = (peer_ids[None, None, :] * N_SUB + own_sub[None, :, None]) * BPD + picked
    return jnp.where(is_live, targets, -1).astype(jnp.int32)


def draw_embeddings(key, part):
    key_center, key_topic, key_noise, key_amp, key_scale, key_offset, key_rows = jax.random.split(key, 7)
    centers = jnp.clip(jax.random.normal(key_center, (N_CLUS, D), jnp.float32), -5.0, 5.0)
    block_ids = jnp.arange(NBLK, dtype=jnp.int32)
    block_clus = block_ids // (BPD * N_SUB)
    topic_shift = jax.random.randint(key_topic, (NBLK, BLK), 0, 3)
    topic_ids = (block_clus[:, None] + topic_shift) % N_CLUS
    strength = jax.random.uniform(key_amp, (NBLK, BLK, 1), jnp.float32, 0.3, 2.5)
    feature_scale = jnp.exp(jax.random.uniform(key_scale, (D,), jnp.float32, 0.0, 2.302585))
    offsets = jnp.clip(jax.random.normal(key_offset, (D,), jnp.float32), -5.0, 5.0)
    rising = 1.0 + 2.0 * block_ids.astype(jnp.float32) / max(NBLK - 1, 1)
    row_scale = jnp.exp(jax.random.uniform(key_rows, (NBLK, BLK, 1), jnp.float32, 0.0, 2.302585))
    noise_part = jnp.clip(jax.random.normal(key_noise, (NBLK, BLK, D), jnp.float32), -5.0, 5.0)
    signal = row_scale * (strength * centers[topic_ids] + noise_part)
    return (feature_scale * signal + offsets * rising[:, None, None]).astype(jnp.bfloat16)


def touch_ends(array, key, low, largest):
    spot = [jax.random.randint(jax.random.fold_in(key, axis), (), 0, length) for axis, length in enumerate(array.shape)]
    widest = array.shape.index(max(array.shape))
    next_to = spot[:widest] + [(spot[widest] + 1) % array.shape[widest]] + spot[widest + 1:]
    return array.at[tuple(spot)].set(low).at[tuple(next_to)].set(largest)


def setup_inputs(seed: int = 0, part: int = 0) -> dict:
    arg_keys = jax.random.split(jax.random.key(seed), 4)
    own_keys = jax.random.split(jax.random.fold_in(arg_keys[3], part), 4)
    embeddings = draw_embeddings(jax.random.fold_in(jax.random.fold_in(arg_keys[3], part), 71), part)
    counts = touch_ends(jax.random.randint(own_keys[1], (NBLK,), BLK // 4, BLK + 1), jax.random.fold_in(own_keys[1], 1), BLK // 4, BLK).astype(jnp.int32)
    partner = draw_partner(jax.random.fold_in(jax.random.fold_in(arg_keys[3], part), 71), part)
    return {"embeddings": embeddings, "counts": counts, "partner": partner}


kernel_beta = 4.0

def standardize(embeddings, counts):
    row_mask = (lax.broadcasted_iota(jnp.int32, (NBLK, BLK), 1) < counts[:, None]).astype(jnp.float32)
    values = embeddings.astype(jnp.float32)
    valid_total = jnp.sum(row_mask)
    feature_mean = lax.optimization_barrier(jnp.sum(values * row_mask[:, :, None], axis=(0, 1))) / valid_total
    centered = values - feature_mean
    spread = lax.optimization_barrier(jnp.sum(centered * centered * row_mask[:, :, None], axis=(0, 1))) / valid_total
    scaled = centered * lax.rsqrt(spread + 1e-05)
    grouping_row_count = scaled * lax.rsqrt(lax.optimization_barrier(jnp.sum(scaled * scaled, axis=2, keepdims=True)) + 1e-06)
    return (grouping_row_count.astype(jnp.bfloat16), row_mask)

def reference(embeddings, counts, partner):
    grouping_row_count, row_mask = standardize(embeddings, counts)
    off_diagonal = 1.0 - jnp.eye(BLK, dtype=jnp.float32)

    def own_block(pair_item):
        block_grouping, block_mask = pair_item
        similarity_matrix = jnp.dot(block_grouping, block_grouping.T, preferred_element_type=jnp.float32)
        kernel = jnp.exp(kernel_beta * (similarity_matrix - 1.0)) * block_mask[:, None] * block_mask[None, :] * off_diagonal
        return lax.optimization_barrier(jnp.sum(kernel, axis=1))
    density = lax.map(own_block, (grouping_row_count, row_mask))
    slot_count = partner.shape[1]
    owners = jnp.broadcast_to((jnp.arange(slot_count, dtype=jnp.int32) // N_REP)[None, :, None], partner.shape).reshape(-1)
    targets = partner.reshape(-1)

    def visiting_position(density, slot_item):
        owner_index, target = slot_item

        def pair_work(current):
            first_block = (owner_index * BPD).astype(jnp.int32)
            cluster_rows = lax.dynamic_slice_in_dim(grouping_row_count, first_block, BPD, 0).reshape(BPD * BLK, D)
            cluster_mask = lax.dynamic_slice_in_dim(row_mask, first_block, BPD, 0).reshape(BPD * BLK)
            safe_target = jnp.maximum(target, 0).astype(jnp.int32)
            partner_rows = lax.dynamic_index_in_dim(grouping_row_count, safe_target, 0, keepdims=False)
            partner_mask = lax.dynamic_index_in_dim(row_mask, safe_target, 0, keepdims=False)
            similarity_matrix = jnp.dot(cluster_rows, partner_rows.T, preferred_element_type=jnp.float32)
            kernel = jnp.exp(kernel_beta * (similarity_matrix - 1.0)) * cluster_mask[:, None] * partner_mask[None, :]
            gained = lax.dynamic_slice_in_dim(current, first_block, BPD, 0) + lax.optimization_barrier(jnp.sum(kernel, axis=1)).reshape(BPD, BLK)
            current = lax.dynamic_update_slice_in_dim(current, gained, first_block, 0)
            column_gain = lax.dynamic_index_in_dim(current, safe_target, 0, keepdims=False) + lax.optimization_barrier(jnp.sum(kernel, axis=0))
            return lax.dynamic_update_index_in_dim(current, column_gain, safe_target, 0)
        return (lax.cond(target >= 0, pair_work, lambda current: current, density), None)
    density = lax.scan(visiting_position, density, (owners, targets))[0]
    row_valid = row_mask > 0
    return jnp.where(row_valid, jnp.log(jnp.where(row_valid, density, 1.0)), 0.0)
```

```python
import functools

import jax
import jax.numpy as jnp
from jax import lax
from jax.experimental import pallas as pl
from jax.experimental.pallas import tpu as pltpu
from jax.sharding import PartitionSpec as P

kernel_beta = 4.0
MESH = pl.DeviceIdType.MESH


def body(
    dims,
    x_hbm,
    counts,
    mine,
    requests_in,
    out,
    x,
    unit,
    stage,
    incoming,
    stats,
    asked,
    asked_s,
    back_out,
    back_in,
    dens,
    dens_peer,
    mean_ref,
    rstd_ref,
    masks,
    x_sem,
    s_sem,
    ask_send,
    ask_recv,
    blk_send,
    blk_recv,
    st_send,
    st_recv,
    back_send,
    back_recv,
    rep_send,
    rep_recv,
):
    nc, ns, nb = dims
    blocks, rows, feats = x.shape
    clusters = nc * ns
    me_c = lax.axis_index("clus")
    me_s = lax.axis_index("sub")
    me_r = lax.axis_index("rep")
    me = me_c * ns + me_s
    mate = 1 - me_r
    f32 = jnp.float32

    load_x = pltpu.make_async_copy(x_hbm, x, x_sem)
    load_x.start()

    barrier = pltpu.get_barrier_semaphore()

    def greet(j, carry):
        q = lax.rem(me + j, clusters)
        pl.semaphore_signal(
            barrier,
            inc=1,
            device_id={"clus": lax.div(q, ns), "sub": lax.rem(q, ns)},
            device_id_type=MESH,
        )
        return carry

    lax.fori_loop(1, clusters, greet, 0)
    pl.semaphore_signal(barrier, inc=1, device_id={"rep": mate}, device_id_type=MESH)
    pl.semaphore_wait(barrier, clusters)

    def ask_copy(peer, slot):
        return pltpu.make_async_remote_copy(
            src_ref=requests_in,
            dst_ref=asked.at[slot],
            send_sem=ask_send.at[peer],
            recv_sem=ask_recv.at[slot],
            device_id={"clus": peer},
            device_id_type=MESH,
        )

    def ask(j, carry):
        ask_copy(lax.rem(me_c + j, nc), me_c).start()
        return carry

    lax.fori_loop(1, nc, ask, 0)
    asked[me_c] = jnp.full(asked.shape[1:], -1, jnp.int32)

    def ask_wait(j, carry):
        p = lax.rem(me_c + j, nc)
        ask_copy(p, p).wait_recv()
        return carry

    lax.fori_loop(1, nc, ask_wait, 0)
    to_s = pltpu.make_async_copy(asked, asked_s, s_sem)
    to_s.start()
    load_x.wait()
    to_s.wait()

    def blk_copy(t, peer, slot):
        return pltpu.make_async_remote_copy(
            src_ref=stage.at[t * nc + peer],
            dst_ref=incoming.at[t * nc + slot],
            send_sem=blk_send.at[t * nc + peer],
            recv_sem=blk_recv.at[t * nc + slot],
            device_id={"clus": peer},
            device_id_type=MESH,
        )

    def serve(k, carry):
        t = lax.div(k, nc - 1)
        peer = lax.rem(me_c + 1 + lax.rem(k, nc - 1), nc)
        want = lax.rem(jnp.maximum(asked_s[peer, t, me_c], 0), blocks)
        stage[t * nc + peer] = x[want]
        blk_copy(t, peer, me_c).start()
        return carry

    lax.fori_loop(0, nb * (nc - 1), serve, 0)

    chunk = 64
    per = rows // chunk
    sub_iota = lax.broadcasted_iota(jnp.int32, (chunk, 1), 0)

    def load(k):
        b = lax.div(k, per)
        c = lax.rem(k, per)
        v = x[b, pl.ds(pl.multiple_of(c * chunk, chunk), chunk), :].astype(f32)
        live = sub_iota + c * chunk < counts[me * blocks + b]
        return v, live

    def add_rows(k, acc):
        v, live = load(k)
        return acc + jnp.where(live, v, 0.0).reshape(chunk // 8, 8, feats).sum(axis=0)

    zero_acc = jnp.zeros((8, feats), f32)
    total = jnp.sum(
        lax.fori_loop(0, blocks * per, add_rows, zero_acc), axis=0, keepdims=True
    )

    def count_of(i):
        return lax.fori_loop(
            0, blocks, lambda b, a: a + counts[i * blocks + b], jnp.int32(0)
        ).astype(f32)

    local_mean = total / count_of(me)

    def add_squares(k, acc):
        v, live = load(k)
        d = jnp.where(live, v - local_mean, 0.0)
        return acc + (d * d).reshape(chunk // 8, 8, feats).sum(axis=0)

    squares = jnp.sum(
        lax.fori_loop(0, blocks * per, add_squares, zero_acc), axis=0, keepdims=True
    )
    stats[me, 0:1, :] = total
    stats[me, 1:2, :] = squares

    def st_copy(q, slot):
        return pltpu.make_async_remote_copy(
            src_ref=stats.at[me],
            dst_ref=stats.at[slot],
            send_sem=st_send.at[q],
            recv_sem=st_recv.at[slot],
            device_id={"clus": lax.div(q, ns), "sub": lax.rem(q, ns)},
            device_id_type=MESH,
        )

    def st_start(j, carry):
        st_copy(lax.rem(me + j, clusters), me).start()
        return carry

    lax.fori_loop(1, clusters, st_start, 0)

    lane = lax.broadcasted_iota(jnp.int32, (1, rows), 1)

    def own_mask(b, carry):
        masks[b] = (lane < counts[me * blocks + b]).astype(f32)
        dens[b] = jnp.zeros((1, rows), f32)
        return carry

    lax.fori_loop(0, blocks, own_mask, 0)

    def st_wait(j, carry):
        q = lax.rem(me + j, clusters)
        st_copy(q, q).wait_recv()
        return carry

    lax.fori_loop(1, clusters, st_wait, 0)

    zero_row = jnp.zeros((1, feats), f32)
    row_total = lax.fori_loop(
        0, clusters, lambda i, a: a + count_of(i), jnp.float32(0.0)
    )
    mean = (
        lax.fori_loop(0, clusters, lambda i, a: a + stats[i, 0:1, :], zero_row)
        / row_total
    )

    def merge(i, a):
        n = count_of(i)
        d = stats[i, 0:1, :] / n - mean
        return a + (stats[i, 1:2, :] + n * (d * d))

    spread = lax.fori_loop(0, clusters, merge, zero_row) / row_total
    mean_ref[...] = mean
    rstd_ref[...] = lax.rsqrt(spread + 1e-05)

    part = 32

    def standardize(src, dst, b, d):
        def some(c, carry):
            at = pl.ds(pl.multiple_of(c * part, part), part)
            s = (src[b, at, :].astype(f32) - mean_ref[...]) * rstd_ref[...]
            r = lax.rsqrt(jnp.sum(s * s, axis=1, keepdims=True) + 1e-06)
            dst[d, at, :] = (s * r).astype(jnp.bfloat16)
            return carry

        lax.fori_loop(0, rows // part, some, 0)

    def own_unit(b, carry):
        standardize(x, unit, b, b)
        return carry

    lax.fori_loop(0, blocks, own_unit, 0)

    def sims(a, b):
        s = lax.dot_general(
            a, b, (((1,), (1,)), ((), ())), preferred_element_type=f32
        )
        return jnp.exp(kernel_beta * (s - 1.0))

    col_iota = lax.broadcasted_iota(jnp.int32, (rows, 1), 0)

    def diagonal(j, carry):
        b = j * 2 + me_r
        block = unit[b]
        e = sims(block, block)
        keep = (col_iota < counts[me * blocks + b]) & (col_iota != lane)
        e = jnp.where(keep, e, 0.0)
        dens[b] = jnp.sum(e, axis=0, keepdims=True) * masks[b]
        return carry

    lax.fori_loop(0, blocks // 2, diagonal, 0)

    def back_copy(t, peer, slot):
        return pltpu.make_async_remote_copy(
            src_ref=back_out.at[t * nc + peer],
            dst_ref=back_in.at[t * nc + slot],
            send_sem=back_send.at[t * nc + peer],
            recv_sem=back_recv.at[t * nc + slot],
            device_id={"clus": peer},
            device_id_type=MESH,
        )

    def pair(k, carry):
        t = lax.div(k, nc - 1)
        p = lax.rem(me_c + nc - 1 - lax.rem(k, nc - 1), nc)
        slot = t * nc + p
        blk_copy(t, p, p).wait_recv()
        standardize(incoming, incoming, slot, slot)
        target = mine[t, p]
        count = jnp.where(target >= 0, counts[jnp.maximum(target, 0)], 0)
        keep = (col_iota < count).astype(f32)
        block = incoming[slot]

        def one(b, acc):
            e = sims(block, unit[b]) * masks[b] * keep
            dens[b] += jnp.sum(e, axis=0, keepdims=True)
            return acc + e

        acc = lax.fori_loop(0, blocks, one, jnp.zeros((rows, rows), f32))
        back_out[slot] = jnp.sum(acc.T, axis=0, keepdims=True)
        back_copy(t, p, me_c).start()
        return carry

    lax.fori_loop(0, nb * (nc - 1), pair, 0)

    def credit(k, carry):
        t = lax.div(k, nc - 1)
        p = lax.rem(me_c + 1 + lax.rem(k, nc - 1), nc)
        back_copy(t, p, p).wait_recv()
        want = asked_s[p, t, me_c]
        want = jnp.where(want >= 0, lax.rem(jnp.maximum(want, 0), blocks), -1)
        got = back_in[t * nc + p]

        def one(b, inner):
            dens[b] += jnp.where(want == b, got, 0.0)
            return inner

        lax.fori_loop(0, blocks, one, 0)
        return carry

    lax.fori_loop(0, nb * (nc - 1), credit, 0)

    share = pltpu.make_async_remote_copy(
        src_ref=dens,
        dst_ref=dens_peer,
        send_sem=rep_send,
        recv_sem=rep_recv,
        device_id={"rep": mate},
        device_id_type=MESH,
    )
    share.start()

    def drain(k, carry):
        t = lax.div(k, nc - 1)
        p = lax.rem(me_c + 1 + lax.rem(k, nc - 1), nc)
        blk_copy(t, p, p).wait_send()
        back_copy(t, p, p).wait_send()
        return carry

    lax.fori_loop(0, nb * (nc - 1), drain, 0)

    def drain_ask(j, carry):
        p = lax.rem(me_c + j, nc)
        ask_copy(p, p).wait_send()
        return carry

    lax.fori_loop(1, nc, drain_ask, 0)

    def drain_st(j, carry):
        q = lax.rem(me + j, clusters)
        st_copy(q, q).wait_send()
        return carry

    lax.fori_loop(1, clusters, drain_st, 0)
    share.wait()

    def finish(b, carry):
        live = masks[b] > 0
        both = jnp.where(live, dens[b] + dens_peer[b], 1.0)
        out[b] = jnp.where(live, jnp.log(both), 0.0)
        return carry

    lax.fori_loop(0, blocks, finish, 0)


def on_device(embeddings, counts, partner):
    blocks, rows, feats = embeddings.shape
    nc, ns = lax.axis_size("clus"), lax.axis_size("sub")
    nb = partner.shape[0]
    lists = partner[:, 0, :]
    requests = jnp.pad(
        lists, ((0, -nb % 8), (0, -nc % 128)), constant_values=-1
    )
    f32, bf16 = jnp.float32, jnp.bfloat16
    dma = pltpu.SemaphoreType.DMA
    vmem = pl.BlockSpec(memory_space=pltpu.VMEM)
    smem = pl.BlockSpec(memory_space=pltpu.SMEM)
    out = pl.pallas_call(
        functools.partial(body, (nc, ns, nb)),
        out_shape=jax.ShapeDtypeStruct((blocks, 1, rows), f32),
        in_specs=[pl.BlockSpec(memory_space=pl.ANY), smem, smem, vmem],
        out_specs=vmem,
        scratch_shapes=[
            pltpu.VMEM((blocks, rows, feats), bf16),
            pltpu.VMEM((blocks, rows, feats), bf16),
            pltpu.VMEM((nb * nc, rows, feats), bf16),
            pltpu.VMEM((nb * nc, rows, feats), bf16),
            pltpu.VMEM((nc * ns, 2, feats), f32),
            pltpu.VMEM((nc,) + requests.shape, jnp.int32),
            pltpu.SMEM((nc,) + requests.shape, jnp.int32),
            pltpu.VMEM((nb * nc, 1, rows), f32),
            pltpu.VMEM((nb * nc, 1, rows), f32),
            pltpu.VMEM((blocks, 1, rows), f32),
            pltpu.VMEM((blocks, 1, rows), f32),
            pltpu.VMEM((1, feats), f32),
            pltpu.VMEM((1, feats), f32),
            pltpu.VMEM((blocks, 1, rows), f32),
            dma,
            dma,
            dma((nc,)),
            dma((nc,)),
            dma((nb * nc,)),
            dma((nb * nc,)),
            dma((nc * ns,)),
            dma((nc * ns,)),
            dma((nb * nc,)),
            dma((nb * nc,)),
            dma,
            dma,
        ],
        compiler_params=pltpu.CompilerParams(
            collective_id=0, has_side_effects=True, vmem_limit_bytes=56 * 2**20
        ),
    )(embeddings, counts, lists, requests)
    return out.reshape(blocks, rows)


def solution(mesh):
    in_specs = (
        P(("groups", "clus", "sub"), None, None),
        P("groups"),
        P(None, ("groups", "clus", "sub", "rep"), None),
    )
    out_specs = P(("groups", "clus", "sub"), None)
    return jax.shard_map(
        on_device, mesh=mesh, in_specs=in_specs, out_specs=out_specs, check_vma=False
    )
```

```python
import functools
import math

import jax
import jax.numpy as jnp
from jax import lax
from jax.experimental import pallas as pl
from jax.experimental.pallas import tpu as pltpu
from jax.sharding import PartitionSpec as P

kernel_beta = 4.0
MESH = pl.DeviceIdType.MESH


def body(
    dims,
    x_hbm,
    counts,
    mine,
    requests_in,
    out,
    x,
    unit,
    stage,
    incoming,
    stats,
    asked,
    asked_s,
    back_out,
    back_in,
    dens,
    dens_peer,
    mean_ref,
    rstd_ref,
    masks,
    x_sem,
    s_sem,
    ask_send,
    ask_recv,
    blk_send,
    blk_recv,
    st_send,
    st_recv,
    back_send,
    back_recv,
    rep_send,
    rep_recv,
):
    nc, ns, nb = dims
    blocks, rows, feats = x.shape
    clusters = nc * ns
    me_c = lax.axis_index("clus")
    me_s = lax.axis_index("sub")
    me_r = lax.axis_index("rep")
    me = me_c * ns + me_s
    mate = 1 - me_r
    f32 = jnp.float32

    load_x = pltpu.make_async_copy(x_hbm, x, x_sem)
    load_x.start()

    barrier = pltpu.get_barrier_semaphore()

    def greet(j, carry):
        q = lax.rem(me + j, clusters)
        pl.semaphore_signal(
            barrier,
            inc=1,
            device_id={"clus": lax.div(q, ns), "sub": lax.rem(q, ns)},
            device_id_type=MESH,
        )
        return carry

    lax.fori_loop(1, clusters, greet, 0)
    pl.semaphore_signal(barrier, inc=1, device_id={"rep": mate}, device_id_type=MESH)
    pl.semaphore_wait(barrier, clusters)

    def ask_copy(peer, slot):
        return pltpu.make_async_remote_copy(
            src_ref=requests_in,
            dst_ref=asked.at[slot],
            send_sem=ask_send.at[peer],
            recv_sem=ask_recv.at[slot],
            device_id={"clus": peer},
            device_id_type=MESH,
        )

    def ask(j, carry):
        ask_copy(lax.rem(me_c + j, nc), me_c).start()
        return carry

    lax.fori_loop(1, nc, ask, 0)
    asked[me_c] = jnp.full(asked.shape[1:], -1, jnp.int32)

    def ask_wait(j, carry):
        p = lax.rem(me_c + j, nc)
        ask_copy(p, p).wait_recv()
        return carry

    lax.fori_loop(1, nc, ask_wait, 0)
    to_s = pltpu.make_async_copy(asked, asked_s, s_sem)
    to_s.start()
    load_x.wait()
    to_s.wait()

    def blk_copy(t, peer, slot):
        return pltpu.make_async_remote_copy(
            src_ref=stage.at[t * nc + peer],
            dst_ref=incoming.at[t * nc + slot],
            send_sem=blk_send.at[t * nc + peer],
            recv_sem=blk_recv.at[t * nc + slot],
            device_id={"clus": peer},
            device_id_type=MESH,
        )

    steps = nb * (nc - 1)
    window = min(4, steps)
    half = nc // 2
    paired = nc & (nc - 1) == 0

    def step(k):
        t = lax.div(k, nc - 1)
        i = lax.rem(k, nc - 1)
        if not paired:
            return t, lax.rem(me_c + 1 + i, nc), lax.rem(me_c + nc - 1 - i, nc)
        early = jnp.where(t == nb - 1, half - 1, half)
        j = jnp.where(i < early, half + i, i - early + 1)
        j = jnp.where((t == nb - 1) & (i == nc - 2), nc - 1, j)
        peer = me_c
        bit = 1
        while bit < nc:
            peer = peer + lax.rem(lax.div(j, bit), 2) * (
                bit - 2 * bit * lax.rem(lax.div(me_c, bit), 2)
            )
            bit *= 2
        return t, peer, peer

    def serve(k, carry):
        t, peer, _ = step(k)
        want = lax.rem(jnp.maximum(asked_s[peer, t, me_c], 0), blocks)
        stage[t * nc + peer] = x[want]
        blk_copy(t, peer, me_c).start()
        return carry

    lax.fori_loop(0, window, serve, 0)

    chunk = 64
    per = rows // chunk
    sub_iota = lax.broadcasted_iota(jnp.int32, (chunk, 1), 0)

    def load(k):
        b = lax.div(k, per)
        c = lax.rem(k, per)
        v = x[b, pl.ds(pl.multiple_of(c * chunk, chunk), chunk), :].astype(f32)
        live = sub_iota + c * chunk < counts[me * blocks + b]
        return v, live

    def add_rows(k, acc):
        v, live = load(k)
        return acc + jnp.where(live, v, 0.0).reshape(chunk // 8, 8, feats).sum(axis=0)

    zero_acc = jnp.zeros((8, feats), f32)
    total = jnp.sum(
        lax.fori_loop(0, blocks * per, add_rows, zero_acc), axis=0, keepdims=True
    )

    def count_of(i):
        return lax.fori_loop(
            0, blocks, lambda b, a: a + counts[i * blocks + b], jnp.int32(0)
        ).astype(f32)

    local_mean = total / count_of(me)

    def add_squares(k, acc):
        v, live = load(k)
        d = jnp.where(live, v - local_mean, 0.0)
        return acc + (d * d).reshape(chunk // 8, 8, feats).sum(axis=0)

    squares = jnp.sum(
        lax.fori_loop(0, blocks * per, add_squares, zero_acc), axis=0, keepdims=True
    )
    stats[me, 0:1, :] = total
    stats[me, 1:2, :] = squares

    def st_copy(q, slot):
        return pltpu.make_async_remote_copy(
            src_ref=stats.at[me],
            dst_ref=stats.at[slot],
            send_sem=st_send.at[q],
            recv_sem=st_recv.at[slot],
            device_id={"clus": lax.div(q, ns), "sub": lax.rem(q, ns)},
            device_id_type=MESH,
        )

    def st_start(j, carry):
        st_copy(lax.rem(me + j, clusters), me).start()
        return carry

    lax.fori_loop(1, clusters, st_start, 0)

    lane = lax.broadcasted_iota(jnp.int32, (1, rows), 1)
    log2_beta = kernel_beta / math.log(2.0)

    def own_mask(b, carry):
        masks[b] = jnp.where(lane < counts[me * blocks + b], -log2_beta, -1e30)
        dens[b] = jnp.zeros((1, rows), f32)
        return carry

    lax.fori_loop(0, blocks, own_mask, 0)

    def st_wait(j, carry):
        q = lax.rem(me + j, clusters)
        st_copy(q, q).wait_recv()
        return carry

    lax.fori_loop(1, clusters, st_wait, 0)

    zero_row = jnp.zeros((1, feats), f32)
    row_total = lax.fori_loop(
        0, clusters, lambda i, a: a + count_of(i), jnp.float32(0.0)
    )
    mean = (
        lax.fori_loop(0, clusters, lambda i, a: a + stats[i, 0:1, :], zero_row)
        / row_total
    )

    def merge(i, a):
        n = count_of(i)
        d = stats[i, 0:1, :] / n - mean
        return a + (stats[i, 1:2, :] + n * (d * d))

    spread = lax.fori_loop(0, clusters, merge, zero_row) / row_total
    mean_ref[...] = mean
    rstd_ref[...] = lax.rsqrt(spread + 1e-05)

    part = 32

    def standardize(src, dst, b, d):
        def some(c, carry):
            at = pl.ds(pl.multiple_of(c * part, part), part)
            s = (src[b, at, :].astype(f32) - mean_ref[...]) * rstd_ref[...]
            r = lax.rsqrt(jnp.sum(s * s, axis=1, keepdims=True) + 1e-06)
            dst[d, at, :] = (s * r).astype(jnp.bfloat16)
            return carry

        lax.fori_loop(0, rows // part, some, 0, unroll=2)

    def own_unit(b, carry):
        standardize(x, unit, b, b)
        return carry

    lax.fori_loop(0, blocks, own_unit, 0)

    def sims(a, b, bias):
        s = lax.dot_general(
            a, b, (((1,), (1,)), ((), ())), preferred_element_type=f32
        )
        return jnp.exp2(log2_beta * s + bias)

    col_iota = lax.broadcasted_iota(jnp.int32, (rows, 1), 0)

    def diagonal(j, carry):
        b = j * 2 + me_r
        block = unit[b]
        e = sims(block, block, masks[b])
        keep = (col_iota < counts[me * blocks + b]) & (col_iota != lane)
        e = jnp.where(keep, e, 0.0)
        dens[b] = jnp.sum(e, axis=0, keepdims=True)
        return carry

    lax.fori_loop(0, blocks // 2, diagonal, 0, unroll=2)

    def back_copy(t, peer, slot):
        return pltpu.make_async_remote_copy(
            src_ref=back_out.at[t * nc + peer],
            dst_ref=back_in.at[t * nc + slot],
            send_sem=back_send.at[t * nc + peer],
            recv_sem=back_recv.at[t * nc + slot],
            device_id={"clus": peer},
            device_id_type=MESH,
        )

    def pair(k, carry):
        t, peer, p = step(k)
        slot = t * nc + p
        blk_copy(t, p, p).wait_recv()
        blk_copy(t, peer, p).wait_send()

        @pl.when(k + window < steps)
        def _():
            serve(k + window, 0)

        standardize(incoming, incoming, slot, slot)
        target = mine[t, p]
        count = jnp.where(target >= 0, counts[jnp.maximum(target, 0)], 0)
        keep = (col_iota < count).astype(f32)
        block = incoming[slot]

        def one(b, acc):
            e = sims(block, unit[b], masks[b]) * keep
            dens[b] += jnp.sum(e, axis=0, keepdims=True)
            for at in range(0, rows, 128):
                acc = acc + e[:, at : at + 128]
            return acc

        acc = lax.fori_loop(0, blocks, one, jnp.zeros((rows, 128), f32), unroll=2)
        back_out[slot] = jnp.sum(acc.T, axis=0, keepdims=True)
        back_copy(t, p, me_c).start()
        return carry

    lax.fori_loop(0, nb * (nc - 1), pair, 0)

    def credit(k, carry):
        t = lax.div(k, nc - 1)
        p = lax.rem(me_c + 1 + lax.rem(k, nc - 1), nc)
        back_copy(t, p, p).wait_recv()
        want = asked_s[p, t, me_c]
        want = jnp.where(want >= 0, lax.rem(jnp.maximum(want, 0), blocks), -1)
        got = back_in[t * nc + p]

        def one(b, inner):
            dens[b] += jnp.where(want == b, got, 0.0)
            return inner

        lax.fori_loop(0, blocks, one, 0)
        return carry

    lax.fori_loop(0, nb * (nc - 1), credit, 0)

    share = pltpu.make_async_remote_copy(
        src_ref=dens,
        dst_ref=dens_peer,
        send_sem=rep_send,
        recv_sem=rep_recv,
        device_id={"rep": mate},
        device_id_type=MESH,
    )
    share.start()

    def drain(k, carry):
        t = lax.div(k, nc - 1)
        p = lax.rem(me_c + 1 + lax.rem(k, nc - 1), nc)
        back_copy(t, p, p).wait_send()
        return carry

    lax.fori_loop(0, nb * (nc - 1), drain, 0)

    def drain_ask(j, carry):
        p = lax.rem(me_c + j, nc)
        ask_copy(p, p).wait_send()
        return carry

    lax.fori_loop(1, nc, drain_ask, 0)

    def drain_st(j, carry):
        q = lax.rem(me + j, clusters)
        st_copy(q, q).wait_send()
        return carry

    lax.fori_loop(1, clusters, drain_st, 0)
    share.wait()

    def finish(b, carry):
        live = masks[b] > -1e29
        both = jnp.where(live, dens[b] + dens_peer[b], 1.0)
        out[b] = jnp.where(live, jnp.log(both), 0.0)
        return carry

    lax.fori_loop(0, blocks, finish, 0)


def on_device(embeddings, counts, partner):
    blocks, rows, feats = embeddings.shape
    nc, ns = lax.axis_size("clus"), lax.axis_size("sub")
    nb = partner.shape[0]
    lists = partner[:, 0, :]
    requests = jnp.pad(
        lists, ((0, -nb % 8), (0, -nc % 128)), constant_values=-1
    )
    f32, bf16 = jnp.float32, jnp.bfloat16
    dma = pltpu.SemaphoreType.DMA
    vmem = pl.BlockSpec(memory_space=pltpu.VMEM)
    smem = pl.BlockSpec(memory_space=pltpu.SMEM)
    out = pl.pallas_call(
        functools.partial(body, (nc, ns, nb)),
        out_shape=jax.ShapeDtypeStruct((blocks, 1, rows), f32),
        in_specs=[pl.BlockSpec(memory_space=pl.ANY), smem, smem, vmem],
        out_specs=vmem,
        scratch_shapes=[
            pltpu.VMEM((blocks, rows, feats), bf16),
            pltpu.VMEM((blocks, rows, feats), bf16),
            pltpu.VMEM((nb * nc, rows, feats), bf16),
            pltpu.VMEM((nb * nc, rows, feats), bf16),
            pltpu.VMEM((nc * ns, 2, feats), f32),
            pltpu.VMEM((nc,) + requests.shape, jnp.int32),
            pltpu.SMEM((nc,) + requests.shape, jnp.int32),
            pltpu.VMEM((nb * nc, 1, rows), f32),
            pltpu.VMEM((nb * nc, 1, rows), f32),
            pltpu.VMEM((blocks, 1, rows), f32),
            pltpu.VMEM((blocks, 1, rows), f32),
            pltpu.VMEM((1, feats), f32),
            pltpu.VMEM((1, feats), f32),
            pltpu.VMEM((blocks, 1, rows), f32),
            dma,
            dma,
            dma((nc,)),
            dma((nc,)),
            dma((nb * nc,)),
            dma((nb * nc,)),
            dma((nc * ns,)),
            dma((nc * ns,)),
            dma((nb * nc,)),
            dma((nb * nc,)),
            dma,
            dma,
        ],
        compiler_params=pltpu.CompilerParams(
            collective_id=0, has_side_effects=True, vmem_limit_bytes=56 * 2**20
        ),
    )(embeddings, counts, lists, requests)
    return out.reshape(blocks, rows)


def solution(mesh):
    in_specs = (
        P(("groups", "clus", "sub"), None, None),
        P("groups"),
        P(None, ("groups", "clus", "sub", "rep"), None),
    )
    out_specs = P(("groups", "clus", "sub"), None)
    return jax.shard_map(
        on_device, mesh=mesh, in_specs=in_specs, out_specs=out_specs, check_vma=False
    )
```

```python
import functools
import math

import jax
import jax.numpy as jnp
from jax import lax
from jax.experimental import pallas as pl
from jax.experimental.pallas import tpu as pltpu
from jax.sharding import PartitionSpec as P

kernel_beta = 4.0
MESH = pl.DeviceIdType.MESH


def layout(lists, counts, unit_rows, blocks, p, c, nb):
    wants, starts, sizes = [], [], []
    end = jnp.int32(0)
    for t in range(nb):
        for r in range(2):
            q = lists(r, t, p)
            safe = jnp.maximum(q, 0)
            size = lax.div(counts[safe] + unit_rows - 1, unit_rows)
            size = jnp.where(q >= 0, size, 0)
            start = end
            for other, place in zip(wants, starts):
                same = (other == q) & (q >= 0)
                size = jnp.where(same, 0, size)
                start = jnp.where(same, place, start)
            wants.append(q)
            starts.append(start)
            sizes.append(size)
            end = end + size
    return wants, starts, sizes, end


def survey(
    dims,
    counts,
    mine,
    tile,
    out_lists,
    out_need,
    asked,
    asked_s,
    needs,
    s_sem,
    ask_send,
    ask_recv,
    need_send,
    need_recv,
):
    ng, nc, ns, nb, blocks, unit_rows = dims
    me_g = lax.axis_index("groups")
    me_c = lax.axis_index("clus")
    me_s = lax.axis_index("sub")
    me_r = lax.axis_index("rep")
    mate = 1 - me_r
    everyone = ng * nc * ns
    me = (me_g * nc + me_c) * ns + me_s

    def where_is(q):
        return {
            "groups": lax.div(q, nc * ns),
            "clus": lax.rem(lax.div(q, ns), nc),
            "sub": lax.rem(q, ns),
        }

    barrier = pltpu.get_barrier_semaphore()

    def greet(j, carry):
        pl.semaphore_signal(
            barrier,
            inc=1,
            device_id=where_is(lax.rem(me + j, everyone)),
            device_id_type=MESH,
        )
        return carry

    lax.fori_loop(1, everyone, greet, 0)

    def greet_other(j, carry):
        pl.semaphore_signal(
            barrier,
            inc=1,
            device_id={"clus": lax.rem(me_c + j, nc), "rep": mate},
            device_id_type=MESH,
        )
        return carry

    lax.fori_loop(0, nc, greet_other, 0)
    pl.semaphore_wait(barrier, everyone - 1 + nc)

    def ask_copy(peer, r, slot):
        return pltpu.make_async_remote_copy(
            src_ref=tile,
            dst_ref=asked.at[slot],
            send_sem=ask_send.at[peer * 2 + r],
            recv_sem=ask_recv.at[slot],
            device_id={"clus": peer, "rep": r},
            device_id_type=MESH,
        )

    own = me_c * 2 + me_r

    def ask(j, carry):
        q = lax.rem(own + j, 2 * nc)
        ask_copy(lax.div(q, 2), lax.rem(q, 2), own).start()
        return carry

    lax.fori_loop(1, 2 * nc, ask, 0)
    asked[own] = tile[...]

    def ask_wait(j, carry):
        q = lax.rem(own + j, 2 * nc)
        ask_copy(lax.div(q, 2), lax.rem(q, 2), q).wait_recv()
        return carry

    lax.fori_loop(1, 2 * nc, ask_wait, 0)
    to_s = pltpu.make_async_copy(asked, asked_s, s_sem)
    to_s.start()
    to_s.wait()
    out_lists[...] = asked[...]

    def lists(r, t, p):
        return asked_s[me_c * 2 + r, t, p]

    def most(p, need):
        end = layout(lists, counts, unit_rows, blocks, p, me_c, nb)[3]
        return jnp.maximum(need, end)

    need = lax.fori_loop(0, nc, most, jnp.int32(0))
    needs[me] = jnp.full(needs.shape[1:], need, jnp.int32)

    def need_copy(q, slot):
        return pltpu.make_async_remote_copy(
            src_ref=needs.at[me],
            dst_ref=needs.at[slot],
            send_sem=need_send.at[q],
            recv_sem=need_recv.at[slot],
            device_id=where_is(q),
            device_id_type=MESH,
        )

    def need_start(j, carry):
        need_copy(lax.rem(me + j, everyone), me).start()
        return carry

    lax.fori_loop(1, everyone, need_start, 0)

    def need_wait(j, carry):
        q = lax.rem(me + j, everyone)
        need_copy(q, q).wait_recv()
        return carry

    lax.fori_loop(1, everyone, need_wait, 0)
    out_need[...] = jnp.max(needs[...], axis=0)

    def drain_ask(j, carry):
        q = lax.rem(own + j, 2 * nc)
        ask_copy(lax.div(q, 2), lax.rem(q, 2), q).wait_send()
        return carry

    lax.fori_loop(1, 2 * nc, drain_ask, 0)

    def drain_need(j, carry):
        q = lax.rem(me + j, everyone)
        need_copy(q, q).wait_send()
        return carry

    lax.fori_loop(1, everyone, drain_need, 0)


def body(
    dims,
    x_hbm,
    counts,
    asked_s,
    out,
    x,
    unit,
    stage,
    incoming,
    land,
    stats,
    back_out,
    back_in,
    dens,
    dens_peer,
    mean_ref,
    rstd_ref,
    masks,
    x_sem,
    blk_send,
    blk_recv,
    fwd_send,
    fwd_recv,
    st_send,
    st_recv,
    back_send,
    back_recv,
    rep_send,
    rep_recv,
):
    nc, ns, nb, blocks, cap = dims
    feats = x.shape[2]
    ur = x.shape[1]
    bu = x.shape[0] // blocks
    rows = bu * ur
    halves = 2
    cu = cap // (2 * halves)
    clusters = nc * ns
    me_c = lax.axis_index("clus")
    me_s = lax.axis_index("sub")
    me_r = lax.axis_index("rep")
    me = me_c * ns + me_s
    mate = 1 - me_r
    f32 = jnp.float32

    load_x = pltpu.make_async_copy(x_hbm, x, x_sem)
    load_x.start()

    barrier = pltpu.get_barrier_semaphore()

    def greet(j, carry):
        q = lax.rem(me + j, clusters)
        pl.semaphore_signal(
            barrier,
            inc=1,
            device_id={"clus": lax.div(q, ns), "sub": lax.rem(q, ns)},
            device_id_type=MESH,
        )
        return carry

    lax.fori_loop(1, clusters, greet, 0)
    pl.semaphore_signal(barrier, inc=1, device_id={"rep": mate}, device_id_type=MESH)
    pl.semaphore_wait(barrier, clusters)

    load_x.wait()

    def blk_copy(k, peer, slot):
        h = lax.rem(k, halves)
        return pltpu.make_async_remote_copy(
            src_ref=stage.at[peer, pl.ds(h * cu, cu)],
            dst_ref=incoming.at[slot, pl.ds((h * 2 + me_r) * cu, cu)],
            send_sem=blk_send.at[peer * halves + h],
            recv_sem=blk_recv.at[slot * halves + h],
            device_id={"clus": peer},
            device_id_type=MESH,
        )

    def fwd_copy(k, slot, core):
        h = lax.rem(k, halves)
        part_of = incoming.at[slot, pl.ds((h * 2 + core) * cu, cu)]
        return pltpu.make_async_remote_copy(
            src_ref=part_of,
            dst_ref=part_of,
            send_sem=fwd_send.at[slot * halves + h],
            recv_sem=fwd_recv.at[slot * halves + h],
            device_id={"rep": mate},
            device_id_type=MESH,
        )

    steps = halves * (nc - 1)
    window = min(4, steps)
    half = nc // 2
    paired = nc & (nc - 1) == 0

    def step(k):
        i = lax.div(k, halves)
        if not paired:
            return lax.rem(me_c + 1 + i, nc), lax.rem(me_c + nc - 1 - i, nc)
        early = half - 1
        j = jnp.where(i < early, half + i, i - early + 1)
        j = jnp.where(i == nc - 2, nc - 1, j)
        peer = me_c
        bit = 1
        while bit < nc:
            peer = peer + lax.rem(lax.div(j, bit), 2) * (
                bit - 2 * bit * lax.rem(lax.div(me_c, bit), 2)
            )
            bit *= 2
        return peer, peer

    def serve(k, carry):
        peer, _ = step(k)
        h = lax.rem(k, halves)

        def lists(r, t, p):
            return asked_s[peer * 2 + r, t, p]

        wants, starts, sizes, _ = layout(lists, counts, ur, blocks, me_c, peer, nb)
        firsts = [
            lax.rem(jnp.maximum(q, 0), blocks) * bu - start
            for q, start in zip(wants, starts)
        ]

        def pack(u, inner):
            g = (h * 2 + me_r) * cu + u
            source = jnp.int32(0)
            for first, start, size in zip(firsts, starts, sizes):
                source = jnp.where((g >= start) & (g < start + size), first + g, source)
            stage[peer, h * cu + u] = x[source]
            return inner

        lax.fori_loop(0, cu, pack, 0)
        blk_copy(k, peer, me_c).start()
        return carry

    lax.fori_loop(0, window, serve, 0)

    chunk = 64
    per = rows // chunk
    sub_iota = lax.broadcasted_iota(jnp.int32, (chunk, 1), 0)

    def load(k):
        b = lax.div(k, per)
        c = lax.rem(k, per)
        at = pl.ds(b * bu + c * (chunk // ur), chunk // ur)
        v = x[at].astype(f32).reshape(chunk, feats)
        live = sub_iota + c * chunk < counts[me * blocks + b]
        return v, live

    def add_rows(k, acc):
        v, live = load(k)
        return acc + jnp.where(live, v, 0.0).reshape(chunk // 8, 8, feats).sum(axis=0)

    zero_acc = jnp.zeros((8, feats), f32)
    total = jnp.sum(
        lax.fori_loop(0, blocks * per, add_rows, zero_acc), axis=0, keepdims=True
    )

    def count_of(i):
        return lax.fori_loop(
            0, blocks, lambda b, a: a + counts[i * blocks + b], jnp.int32(0)
        ).astype(f32)

    local_mean = total / count_of(me)

    def add_squares(k, acc):
        v, live = load(k)
        d = jnp.where(live, v - local_mean, 0.0)
        return acc + (d * d).reshape(chunk // 8, 8, feats).sum(axis=0)

    squares = jnp.sum(
        lax.fori_loop(0, blocks * per, add_squares, zero_acc), axis=0, keepdims=True
    )
    stats[me, 0:1, :] = total
    stats[me, 1:2, :] = squares

    def st_copy(q, slot):
        return pltpu.make_async_remote_copy(
            src_ref=stats.at[me],
            dst_ref=stats.at[slot],
            send_sem=st_send.at[q],
            recv_sem=st_recv.at[slot],
            device_id={"clus": lax.div(q, ns), "sub": lax.rem(q, ns)},
            device_id_type=MESH,
        )

    def st_start(j, carry):
        st_copy(lax.rem(me + j, clusters), me).start()
        return carry

    lax.fori_loop(1, clusters, st_start, 0)

    lane = lax.broadcasted_iota(jnp.int32, (1, rows), 1)
    log2_beta = kernel_beta / math.log(2.0)

    def own_mask(b, carry):
        masks[b] = jnp.where(lane < counts[me * blocks + b], -log2_beta, -1e30)
        dens[b] = jnp.zeros((1, rows), f32)
        return carry

    lax.fori_loop(0, blocks, own_mask, 0)

    def st_wait(j, carry):
        q = lax.rem(me + j, clusters)
        st_copy(q, q).wait_recv()
        return carry

    lax.fori_loop(1, clusters, st_wait, 0)

    zero_row = jnp.zeros((1, feats), f32)
    row_total = lax.fori_loop(
        0, clusters, lambda i, a: a + count_of(i), jnp.float32(0.0)
    )
    mean = (
        lax.fori_loop(0, clusters, lambda i, a: a + stats[i, 0:1, :], zero_row)
        / row_total
    )

    def merge(i, a):
        n = count_of(i)
        d = stats[i, 0:1, :] / n - mean
        return a + (stats[i, 1:2, :] + n * (d * d))

    spread = lax.fori_loop(0, clusters, merge, zero_row) / row_total
    mean_ref[...] = mean
    rstd_ref[...] = lax.rsqrt(spread + 1e-05)

    part = 2

    def standardize(v):
        s = (v.astype(f32).reshape(part * ur, feats) - mean_ref[...]) * rstd_ref[...]
        r = lax.rsqrt(jnp.sum(s * s, axis=1, keepdims=True) + 1e-06)
        return (s * r).astype(jnp.bfloat16)

    def own_unit(c, carry):
        at = pl.ds(c * part, part)
        unit[at] = standardize(x[at]).reshape(part, ur, feats)
        return carry

    lax.fori_loop(0, blocks * bu // part, own_unit, 0, unroll=2)
    land[pl.ds(cap, bu)] = jnp.zeros((bu, ur, feats), jnp.bfloat16)

    def block_of(ref, at):
        return ref[pl.ds(at, bu)].reshape(rows, feats)

    def sims(a, b, bias):
        s = lax.dot_general(
            a, b, (((1,), (1,)), ((), ())), preferred_element_type=f32
        )
        return jnp.exp2(log2_beta * s + bias)

    col_iota = lax.broadcasted_iota(jnp.int32, (rows, 1), 0)

    def diagonal(j, carry):
        b = j * 2 + me_r
        block = block_of(unit, b * bu)
        e = sims(block, block, masks[b])
        keep = (col_iota < counts[me * blocks + b]) & (col_iota != lane)
        e = jnp.where(keep, e, 0.0)
        dens[b] = jnp.sum(e, axis=0, keepdims=True)
        return carry

    lax.fori_loop(0, blocks // 2, diagonal, 0, unroll=2)

    def back_copy(t, peer, slot):
        return pltpu.make_async_remote_copy(
            src_ref=back_out.at[t * nc + peer],
            dst_ref=back_in.at[t * nc + slot],
            send_sem=back_send.at[t * nc + peer],
            recv_sem=back_recv.at[t * nc + slot],
            device_id={"clus": peer},
            device_id_type=MESH,
        )

    def receive(k, carry):
        peer, p = step(k)
        blk_copy(k, p, p).wait_recv()
        blk_copy(k, peer, p).wait_send()
        fwd_copy(k, p, me_r).start()

        @pl.when(k + window < steps)
        def _():
            serve(k + window, 0)

        return carry

    def pairs(i, carry):
        lax.fori_loop(i * halves, (i + 1) * halves, receive, 0)
        _, p = step(i * halves)

        def arrive(h, inner):
            fwd_copy(h, p, mate).wait_recv()
            return inner

        lax.fori_loop(0, halves, arrive, 0)

        def unit_part(c, inner):
            at = pl.ds(c * part, part)
            land[at] = standardize(incoming[p, at]).reshape(part, ur, feats)
            return inner

        lax.fori_loop(0, cap // part, unit_part, 0, unroll=2)

        def lists(r, t, q):
            return asked_s[me_c * 2 + r, t, q]

        wants, starts, _, _ = layout(lists, counts, ur, blocks, p, me_c, nb)
        for t in range(nb):
            target = jnp.where(me_r == 0, wants[2 * t], wants[2 * t + 1])
            start = jnp.where(me_r == 0, starts[2 * t], starts[2 * t + 1])
            count = jnp.where(target >= 0, counts[jnp.maximum(target, 0)], 0)
            keep = (col_iota < count).astype(f32)
            block = block_of(land, start)

            def one(b, acc):
                e = sims(block, block_of(unit, b * bu), masks[b]) * keep
                dens[b] += jnp.sum(e, axis=0, keepdims=True)
                for at in range(0, rows, 128):
                    acc = acc + e[:, at : at + 128]
                return acc

            acc = lax.fori_loop(
                0, blocks, one, jnp.zeros((rows, 128), f32), unroll=2
            )
            back_out[t * nc + p] = jnp.sum(acc.T, axis=0, keepdims=True)
            back_copy(t, p, me_c).start()
        return carry

    lax.fori_loop(0, nc - 1, pairs, 0)

    def credit(k, carry):
        t = lax.div(k, nc - 1)
        p = lax.rem(me_c + 1 + lax.rem(k, nc - 1), nc)
        back_copy(t, p, p).wait_recv()
        want = asked_s[p * 2 + me_r, t, me_c]
        want = jnp.where(want >= 0, lax.rem(jnp.maximum(want, 0), blocks), -1)
        got = back_in[t * nc + p]

        def one(b, inner):
            dens[b] += jnp.where(want == b, got, 0.0)
            return inner

        lax.fori_loop(0, blocks, one, 0)
        return carry

    lax.fori_loop(0, nb * (nc - 1), credit, 0)

    share = pltpu.make_async_remote_copy(
        src_ref=dens,
        dst_ref=dens_peer,
        send_sem=rep_send,
        recv_sem=rep_recv,
        device_id={"rep": mate},
        device_id_type=MESH,
    )
    share.start()

    def drain(k, carry):
        t = lax.div(k, nc - 1)
        p = lax.rem(me_c + 1 + lax.rem(k, nc - 1), nc)
        back_copy(t, p, p).wait_send()
        return carry

    lax.fori_loop(0, nb * (nc - 1), drain, 0)

    def drain_fwd(k, carry):
        _, p = step(k)
        fwd_copy(k, p, me_r).wait_send()
        return carry

    lax.fori_loop(0, steps, drain_fwd, 0)

    def drain_st(j, carry):
        q = lax.rem(me + j, clusters)
        st_copy(q, q).wait_send()
        return carry

    lax.fori_loop(1, clusters, drain_st, 0)
    share.wait()

    def finish(b, carry):
        live = masks[b] > -1e29
        both = jnp.where(live, dens[b] + dens_peer[b], 1.0)
        out[b] = jnp.where(live, jnp.log(both), 0.0)
        return carry

    lax.fori_loop(0, blocks, finish, 0)


def on_device(embeddings, counts, partner):
    blocks, rows, feats = embeddings.shape
    ng, nc, ns = (lax.axis_size(a) for a in ("groups", "clus", "sub"))
    nb = partner.shape[0]
    ur = 16
    bu = rows // ur
    lists = partner[:, 0, :]
    tile = jnp.pad(lists, ((0, -nb % 8), (0, -nc % 128)), constant_values=-1)
    f32, bf16 = jnp.float32, jnp.bfloat16
    dma = pltpu.SemaphoreType.DMA
    vmem = pl.BlockSpec(memory_space=pltpu.VMEM)
    smem = pl.BlockSpec(memory_space=pltpu.SMEM)
    tiles = jax.ShapeDtypeStruct((2 * nc,) + tile.shape, jnp.int32)
    everyone = ng * nc * ns
    asked, need = pl.pallas_call(
        functools.partial(survey, (ng, nc, ns, nb, blocks, ur)),
        out_shape=(tiles, jax.ShapeDtypeStruct((8, 128), jnp.int32)),
        in_specs=[smem, smem, vmem],
        out_specs=(vmem, vmem),
        scratch_shapes=[
            pltpu.VMEM(tiles.shape, jnp.int32),
            pltpu.SMEM(tiles.shape, jnp.int32),
            pltpu.VMEM((everyone, 8, 128), jnp.int32),
            dma,
            dma((2 * nc,)),
            dma((2 * nc,)),
            dma((everyone,)),
            dma((everyone,)),
        ],
        compiler_params=pltpu.CompilerParams(collective_id=0, has_side_effects=True),
    )(counts, lists, tile)

    most = 2 * nb * bu
    caps = sorted({most * k // 16 // 4 * 4 for k in (9, 10, 11, 12, 14, 16)})

    def with_cap(number, cap):
        def call(x, counts, asked):
            return pl.pallas_call(
                functools.partial(body, (nc, ns, nb, blocks, cap)),
                out_shape=jax.ShapeDtypeStruct((blocks, 1, rows), f32),
                in_specs=[pl.BlockSpec(memory_space=pl.ANY), smem, smem],
                out_specs=vmem,
                scratch_shapes=[
                    pltpu.VMEM((blocks * bu, ur, feats), bf16),
                    pltpu.VMEM((blocks * bu, ur, feats), bf16),
                    pltpu.VMEM((nc, cap // 2, ur, feats), bf16),
                    pltpu.VMEM((nc, cap, ur, feats), bf16),
                    pltpu.VMEM((cap + bu, ur, feats), bf16),
                    pltpu.VMEM((nc * ns, 2, feats), f32),
                    pltpu.VMEM((nb * nc, 1, rows), f32),
                    pltpu.VMEM((nb * nc, 1, rows), f32),
                    pltpu.VMEM((blocks, 1, rows), f32),
                    pltpu.VMEM((blocks, 1, rows), f32),
                    pltpu.VMEM((1, feats), f32),
                    pltpu.VMEM((1, feats), f32),
                    pltpu.VMEM((blocks, 1, rows), f32),
                    dma,
                    dma((2 * nc,)),
                    dma((2 * nc,)),
                    dma((2 * nc,)),
                    dma((2 * nc,)),
                    dma((nc * ns,)),
                    dma((nc * ns,)),
                    dma((nb * nc,)),
                    dma((nb * nc,)),
                    dma,
                    dma,
                ],
                compiler_params=pltpu.CompilerParams(
                    collective_id=1 + number,
                    has_side_effects=True,
                    vmem_limit_bytes=62 * 2**20,
                ),
            )(x, counts, asked)

        return call

    which = sum((need[0, 0] > cap).astype(jnp.int32) for cap in caps[:-1])
    out = lax.switch(
        which,
        [with_cap(number, cap) for number, cap in enumerate(caps)],
        embeddings.reshape(blocks * bu, ur, feats),
        counts,
        asked,
    )
    return out.reshape(blocks, rows)


def solution(mesh):
    in_specs = (
        P(("groups", "clus", "sub"), None, None),
        P("groups"),
        P(None, ("groups", "clus", "sub", "rep"), None),
    )
    out_specs = P(("groups", "clus", "sub"), None)
    return jax.shard_map(
        on_device, mesh=mesh, in_specs=in_specs, out_specs=out_specs, check_vma=False
    )
```

```python
import functools
import math

import jax
import jax.numpy as jnp
from jax import lax
from jax.experimental import pallas as pl
from jax.experimental.pallas import tpu as pltpu
from jax.sharding import PartitionSpec as P

kernel_beta = 4.0
MESH = pl.DeviceIdType.MESH


def layout(lists, counts, unit_rows, blocks, p, c, nb):
    wants, starts, sizes = [], [], []
    end = jnp.int32(0)
    for t in range(nb):
        for r in range(2):
            q = lists(r, t, p)
            safe = jnp.maximum(q, 0)
            size = lax.div(counts[safe] + unit_rows - 1, unit_rows)
            size = jnp.where(q >= 0, size, 0)
            start = end
            for other, place in zip(wants, starts):
                same = (other == q) & (q >= 0)
                size = jnp.where(same, 0, size)
                start = jnp.where(same, place, start)
            wants.append(q)
            starts.append(start)
            sizes.append(size)
            end = end + size
    return wants, starts, sizes, end


def survey(
    dims,
    counts,
    mine,
    tile,
    out_lists,
    out_need,
    asked,
    asked_s,
    needs,
    s_sem,
    ask_send,
    ask_recv,
    need_send,
    need_recv,
):
    ng, nc, ns, nb, blocks, unit_rows = dims
    me_g = lax.axis_index("groups")
    me_c = lax.axis_index("clus")
    me_s = lax.axis_index("sub")
    me_r = lax.axis_index("rep")
    mate = 1 - me_r
    everyone = ng * nc * ns
    me = (me_g * nc + me_c) * ns + me_s

    def others(act):
        def one(j, at):
            g, c, s = at
            s = s + 1
            c = jnp.where(s == ns, c + 1, c)
            s = jnp.where(s == ns, 0, s)
            g = jnp.where(c == nc, g + 1, g)
            c = jnp.where(c == nc, 0, c)
            g = jnp.where(g == ng, 0, g)
            act({"groups": g, "clus": c, "sub": s}, (g * nc + c) * ns + s)
            return g, c, s

        lax.fori_loop(1, everyone, one, (me_g, me_c, me_s))

    barrier = pltpu.get_barrier_semaphore()

    others(
        lambda at, q: pl.semaphore_signal(
            barrier, inc=1, device_id=at, device_id_type=MESH
        )
    )

    def greet_other(j, carry):
        pl.semaphore_signal(
            barrier,
            inc=1,
            device_id={"clus": lax.rem(me_c + j, nc), "rep": mate},
            device_id_type=MESH,
        )
        return carry

    lax.fori_loop(0, nc, greet_other, 0)
    pl.semaphore_wait(barrier, everyone - 1 + nc)

    def ask_copy(peer, r, slot):
        return pltpu.make_async_remote_copy(
            src_ref=tile,
            dst_ref=asked.at[slot],
            send_sem=ask_send.at[peer * 2 + r],
            recv_sem=ask_recv.at[slot],
            device_id={"clus": peer, "rep": r},
            device_id_type=MESH,
        )

    own = me_c * 2 + me_r

    def ask(j, carry):
        q = lax.rem(own + j, 2 * nc)
        ask_copy(lax.div(q, 2), lax.rem(q, 2), own).start()
        return carry

    lax.fori_loop(1, 2 * nc, ask, 0)
    asked[own] = tile[...]

    def ask_wait(j, carry):
        q = lax.rem(own + j, 2 * nc)
        ask_copy(lax.div(q, 2), lax.rem(q, 2), q).wait_recv()
        return carry

    lax.fori_loop(1, 2 * nc, ask_wait, 0)
    to_s = pltpu.make_async_copy(asked, asked_s, s_sem)
    to_s.start()
    to_s.wait()
    out_lists[...] = asked[...]

    def lists(r, t, p):
        return asked_s[me_c * 2 + r, t, p]

    def most(p, need):
        end = layout(lists, counts, unit_rows, blocks, p, me_c, nb)[3]
        return jnp.maximum(need, end)

    need = lax.fori_loop(0, nc, most, jnp.int32(0))
    needs[me] = jnp.full(needs.shape[1:], need, jnp.int32)

    def need_copy(at, q, slot):
        return pltpu.make_async_remote_copy(
            src_ref=needs.at[me],
            dst_ref=needs.at[slot],
            send_sem=need_send.at[q],
            recv_sem=need_recv.at[slot],
            device_id=at,
            device_id_type=MESH,
        )

    others(lambda at, q: need_copy(at, q, me).start())
    others(lambda at, q: need_copy(at, q, q).wait_recv())
    out_need[...] = jnp.max(needs[...], axis=0)

    def drain_ask(j, carry):
        q = lax.rem(own + j, 2 * nc)
        ask_copy(lax.div(q, 2), lax.rem(q, 2), q).wait_send()
        return carry

    lax.fori_loop(1, 2 * nc, drain_ask, 0)

    others(lambda at, q: need_copy(at, q, q).wait_send())


def body(
    dims,
    x_hbm,
    counts,
    asked_s,
    out,
    x,
    unit,
    stage,
    incoming,
    land,
    stats,
    back_out,
    back_in,
    dens,
    dens_peer,
    mean_ref,
    rstd_ref,
    masks,
    x_sem,
    blk_send,
    blk_recv,
    fwd_send,
    fwd_recv,
    st_send,
    st_recv,
    back_send,
    back_recv,
    rep_send,
    rep_recv,
):
    nc, ns, nb, blocks, cap = dims
    feats = x.shape[2]
    ur = x.shape[1]
    bu = x.shape[0] // blocks
    rows = bu * ur
    halves = 2
    cu = cap // (2 * halves)
    clusters = nc * ns
    me_c = lax.axis_index("clus")
    me_s = lax.axis_index("sub")
    me_r = lax.axis_index("rep")
    me = me_c * ns + me_s
    mate = 1 - me_r
    f32 = jnp.float32

    load_x = pltpu.make_async_copy(x_hbm, x, x_sem)
    load_x.start()

    barrier = pltpu.get_barrier_semaphore()

    def greet(j, carry):
        q = lax.rem(me + j, clusters)
        pl.semaphore_signal(
            barrier,
            inc=1,
            device_id={"clus": lax.div(q, ns), "sub": lax.rem(q, ns)},
            device_id_type=MESH,
        )
        return carry

    lax.fori_loop(1, clusters, greet, 0)
    pl.semaphore_signal(barrier, inc=1, device_id={"rep": mate}, device_id_type=MESH)
    pl.semaphore_wait(barrier, clusters)

    load_x.wait()

    def blk_copy(k, peer, slot):
        h = lax.rem(k, halves)
        return pltpu.make_async_remote_copy(
            src_ref=stage.at[peer, pl.ds(h * cu, cu)],
            dst_ref=incoming.at[slot, pl.ds((h * 2 + me_r) * cu, cu)],
            send_sem=blk_send.at[peer * halves + h],
            recv_sem=blk_recv.at[slot * halves + h],
            device_id={"clus": peer},
            device_id_type=MESH,
        )

    def fwd_copy(k, slot, core):
        h = lax.rem(k, halves)
        part_of = incoming.at[slot, pl.ds((h * 2 + core) * cu, cu)]
        return pltpu.make_async_remote_copy(
            src_ref=part_of,
            dst_ref=part_of,
            send_sem=fwd_send.at[slot * halves + h],
            recv_sem=fwd_recv.at[slot * halves + h],
            device_id={"rep": mate},
            device_id_type=MESH,
        )

    steps = halves * (nc - 1)
    window = min(4, steps)
    half = nc // 2
    paired = nc & (nc - 1) == 0

    def step(k):
        i = lax.div(k, halves)
        if not paired:
            return lax.rem(me_c + 1 + i, nc), lax.rem(me_c + nc - 1 - i, nc)
        early = half - 1
        j = jnp.where(i < early, half + i, i - early + 1)
        j = jnp.where(i == nc - 2, nc - 1, j)
        peer = me_c
        bit = 1
        while bit < nc:
            peer = peer + lax.rem(lax.div(j, bit), 2) * (
                bit - 2 * bit * lax.rem(lax.div(me_c, bit), 2)
            )
            bit *= 2
        return peer, peer

    def serve(k, carry):
        peer, _ = step(k)
        h = lax.rem(k, halves)

        def lists(r, t, p):
            return asked_s[peer * 2 + r, t, p]

        wants, starts, sizes, _ = layout(lists, counts, ur, blocks, me_c, peer, nb)
        firsts = [
            lax.rem(jnp.maximum(q, 0), blocks) * bu - start
            for q, start in zip(wants, starts)
        ]

        def pack(u, inner):
            g = (h * 2 + me_r) * cu + u
            source = jnp.int32(0)
            for first, start, size in zip(firsts, starts, sizes):
                source = jnp.where((g >= start) & (g < start + size), first + g, source)
            stage[peer, h * cu + u] = x[source]
            return inner

        lax.fori_loop(0, cu, pack, 0)
        blk_copy(k, peer, me_c).start()
        return carry

    lax.fori_loop(0, window, serve, 0)

    chunk = 64
    per = rows // chunk
    sub_iota = lax.broadcasted_iota(jnp.int32, (chunk, 1), 0)

    def load(k):
        b = lax.div(k, per)
        c = lax.rem(k, per)
        at = pl.ds(b * bu + c * (chunk // ur), chunk // ur)
        v = x[at].astype(f32).reshape(chunk, feats)
        live = sub_iota + c * chunk < counts[me * blocks + b]
        return v, live

    def add_rows(k, acc):
        v, live = load(k)
        return acc + jnp.where(live, v, 0.0).reshape(chunk // 8, 8, feats).sum(axis=0)

    zero_acc = jnp.zeros((8, feats), f32)
    total = jnp.sum(
        lax.fori_loop(0, blocks * per, add_rows, zero_acc), axis=0, keepdims=True
    )

    def count_of(i):
        return lax.fori_loop(
            0, blocks, lambda b, a: a + counts[i * blocks + b], jnp.int32(0)
        ).astype(f32)

    local_mean = total / count_of(me)

    def add_squares(k, acc):
        v, live = load(k)
        d = jnp.where(live, v - local_mean, 0.0)
        return acc + (d * d).reshape(chunk // 8, 8, feats).sum(axis=0)

    squares = jnp.sum(
        lax.fori_loop(0, blocks * per, add_squares, zero_acc), axis=0, keepdims=True
    )
    stats[me, 0:1, :] = total
    stats[me, 1:2, :] = squares

    def st_copy(q, slot):
        return pltpu.make_async_remote_copy(
            src_ref=stats.at[me],
            dst_ref=stats.at[slot],
            send_sem=st_send.at[q],
            recv_sem=st_recv.at[slot],
            device_id={"clus": lax.div(q, ns), "sub": lax.rem(q, ns)},
            device_id_type=MESH,
        )

    def st_start(j, carry):
        st_copy(lax.rem(me + j, clusters), me).start()
        return carry

    lax.fori_loop(1, clusters, st_start, 0)

    lane = lax.broadcasted_iota(jnp.int32, (1, rows), 1)
    log2_beta = kernel_beta / math.log(2.0)

    def own_mask(b, carry):
        masks[b] = jnp.where(lane < counts[me * blocks + b], -log2_beta, -1e30)
        dens[b] = jnp.zeros((1, rows), f32)
        return carry

    lax.fori_loop(0, blocks, own_mask, 0)

    def st_wait(j, carry):
        q = lax.rem(me + j, clusters)
        st_copy(q, q).wait_recv()
        return carry

    lax.fori_loop(1, clusters, st_wait, 0)

    zero_row = jnp.zeros((1, feats), f32)
    row_total = lax.fori_loop(
        0, clusters, lambda i, a: a + count_of(i), jnp.float32(0.0)
    )
    mean = (
        lax.fori_loop(0, clusters, lambda i, a: a + stats[i, 0:1, :], zero_row)
        / row_total
    )

    def merge(i, a):
        n = count_of(i)
        d = stats[i, 0:1, :] / n - mean
        return a + (stats[i, 1:2, :] + n * (d * d))

    spread = lax.fori_loop(0, clusters, merge, zero_row) / row_total
    mean_ref[...] = mean
    rstd_ref[...] = lax.rsqrt(spread + 1e-05)

    part = 2

    def standardize(v):
        s = (v.astype(f32).reshape(part * ur, feats) - mean_ref[...]) * rstd_ref[...]
        r = lax.rsqrt(jnp.sum(s * s, axis=1, keepdims=True) + 1e-06)
        return (s * r).astype(jnp.bfloat16)

    def own_unit(c, carry):
        at = pl.ds(c * part, part)
        unit[at] = standardize(x[at]).reshape(part, ur, feats)
        return carry

    lax.fori_loop(0, blocks * bu // part, own_unit, 0, unroll=2)
    land[pl.ds(cap, bu)] = jnp.zeros((bu, ur, feats), jnp.bfloat16)

    def block_of(ref, at):
        return ref[pl.ds(at, bu)].reshape(rows, feats)

    def sims(a, b, bias):
        s = lax.dot_general(
            a, b, (((1,), (1,)), ((), ())), preferred_element_type=f32
        )
        return jnp.exp2(log2_beta * s + bias)

    col_iota = lax.broadcasted_iota(jnp.int32, (rows, 1), 0)

    def diagonal(j, carry):
        b = j * 2 + me_r
        block = block_of(unit, b * bu)
        e = sims(block, block, masks[b])
        keep = (col_iota < counts[me * blocks + b]) & (col_iota != lane)
        e = jnp.where(keep, e, 0.0)
        dens[b] = jnp.sum(e, axis=0, keepdims=True)
        return carry

    lax.fori_loop(0, blocks // 2, diagonal, 0, unroll=2)

    def back_copy(t, peer, slot):
        return pltpu.make_async_remote_copy(
            src_ref=back_out.at[t * nc + peer],
            dst_ref=back_in.at[t * nc + slot],
            send_sem=back_send.at[t * nc + peer],
            recv_sem=back_recv.at[t * nc + slot],
            device_id={"clus": peer},
            device_id_type=MESH,
        )

    def receive(k, carry):
        peer, p = step(k)
        blk_copy(k, p, p).wait_recv()
        blk_copy(k, peer, p).wait_send()
        fwd_copy(k, p, me_r).start()

        @pl.when(k + window < steps)
        def _():
            serve(k + window, 0)

        return carry

    def pairs(i, carry):
        lax.fori_loop(i * halves, (i + 1) * halves, receive, 0)
        _, p = step(i * halves)

        def arrive(h, inner):
            fwd_copy(h, p, mate).wait_recv()
            return inner

        lax.fori_loop(0, halves, arrive, 0)

        def unit_part(c, inner):
            at = pl.ds(c * part, part)
            land[at] = standardize(incoming[p, at]).reshape(part, ur, feats)
            return inner

        lax.fori_loop(0, cap // part, unit_part, 0, unroll=2)

        def lists(r, t, q):
            return asked_s[me_c * 2 + r, t, q]

        wants, starts, _, _ = layout(lists, counts, ur, blocks, p, me_c, nb)
        for t in range(nb):
            target = jnp.where(me_r == 0, wants[2 * t], wants[2 * t + 1])
            start = jnp.where(me_r == 0, starts[2 * t], starts[2 * t + 1])
            count = jnp.where(target >= 0, counts[jnp.maximum(target, 0)], 0)
            keep = (col_iota < count).astype(f32)
            block = block_of(land, start)

            def one(b, acc):
                e = sims(block, block_of(unit, b * bu), masks[b]) * keep
                dens[b] += jnp.sum(e, axis=0, keepdims=True)
                for at in range(0, rows, 128):
                    acc = acc + e[:, at : at + 128]
                return acc

            acc = lax.fori_loop(
                0, blocks, one, jnp.zeros((rows, 128), f32), unroll=2
            )
            back_out[t * nc + p] = jnp.sum(acc.T, axis=0, keepdims=True)
            back_copy(t, p, me_c).start()
        return carry

    lax.fori_loop(0, nc - 1, pairs, 0)

    def credit(k, carry):
        t = lax.div(k, nc - 1)
        p = lax.rem(me_c + 1 + lax.rem(k, nc - 1), nc)
        back_copy(t, p, p).wait_recv()
        want = asked_s[p * 2 + me_r, t, me_c]
        want = jnp.where(want >= 0, lax.rem(jnp.maximum(want, 0), blocks), -1)
        got = back_in[t * nc + p]

        def one(b, inner):
            dens[b] += jnp.where(want == b, got, 0.0)
            return inner

        lax.fori_loop(0, blocks, one, 0)
        return carry

    lax.fori_loop(0, nb * (nc - 1), credit, 0)

    share = pltpu.make_async_remote_copy(
        src_ref=dens,
        dst_ref=dens_peer,
        send_sem=rep_send,
        recv_sem=rep_recv,
        device_id={"rep": mate},
        device_id_type=MESH,
    )
    share.start()

    def drain(k, carry):
        t = lax.div(k, nc - 1)
        p = lax.rem(me_c + 1 + lax.rem(k, nc - 1), nc)
        back_copy(t, p, p).wait_send()
        return carry

    lax.fori_loop(0, nb * (nc - 1), drain, 0)

    def drain_fwd(k, carry):
        _, p = step(k)
        fwd_copy(k, p, me_r).wait_send()
        return carry

    lax.fori_loop(0, steps, drain_fwd, 0)

    def drain_st(j, carry):
        q = lax.rem(me + j, clusters)
        st_copy(q, q).wait_send()
        return carry

    lax.fori_loop(1, clusters, drain_st, 0)
    share.wait()

    def finish(b, carry):
        live = masks[b] > -1e29
        both = jnp.where(live, dens[b] + dens_peer[b], 1.0)
        out[b] = jnp.where(live, jnp.log(both), 0.0)
        return carry

    lax.fori_loop(0, blocks, finish, 0)


def on_device(embeddings, counts, partner):
    blocks, rows, feats = embeddings.shape
    ng, nc, ns = (lax.axis_size(a) for a in ("groups", "clus", "sub"))
    nb = partner.shape[0]
    ur = 16
    bu = rows // ur
    lists = partner[:, 0, :]
    tile = jnp.pad(lists, ((0, -nb % 8), (0, -nc % 128)), constant_values=-1)
    f32, bf16 = jnp.float32, jnp.bfloat16
    dma = pltpu.SemaphoreType.DMA
    vmem = pl.BlockSpec(memory_space=pltpu.VMEM)
    smem = pl.BlockSpec(memory_space=pltpu.SMEM)
    tiles = jax.ShapeDtypeStruct((2 * nc,) + tile.shape, jnp.int32)
    everyone = ng * nc * ns
    asked, need = pl.pallas_call(
        functools.partial(survey, (ng, nc, ns, nb, blocks, ur)),
        out_shape=(tiles, jax.ShapeDtypeStruct((8, 128), jnp.int32)),
        in_specs=[smem, smem, vmem],
        out_specs=(vmem, vmem),
        scratch_shapes=[
            pltpu.VMEM(tiles.shape, jnp.int32),
            pltpu.SMEM(tiles.shape, jnp.int32),
            pltpu.VMEM((everyone, 8, 128), jnp.int32),
            dma,
            dma((2 * nc,)),
            dma((2 * nc,)),
            dma((everyone,)),
            dma((everyone,)),
        ],
        compiler_params=pltpu.CompilerParams(collective_id=0, has_side_effects=True),
    )(counts, lists, tile)

    most = 2 * nb * bu
    caps = sorted({most * k // 16 // 4 * 4 for k in (9, 10, 11, 12, 14, 16)})

    def with_cap(number, cap):
        def call(x, counts, asked):
            return pl.pallas_call(
                functools.partial(body, (nc, ns, nb, blocks, cap)),
                out_shape=jax.ShapeDtypeStruct((blocks, 1, rows), f32),
                in_specs=[pl.BlockSpec(memory_space=pl.ANY), smem, smem],
                out_specs=vmem,
                scratch_shapes=[
                    pltpu.VMEM((blocks * bu, ur, feats), bf16),
                    pltpu.VMEM((blocks * bu, ur, feats), bf16),
                    pltpu.VMEM((nc, cap // 2, ur, feats), bf16),
                    pltpu.VMEM((nc, cap, ur, feats), bf16),
                    pltpu.VMEM((cap + bu, ur, feats), bf16),
                    pltpu.VMEM((nc * ns, 2, feats), f32),
                    pltpu.VMEM((nb * nc, 1, rows), f32),
                    pltpu.VMEM((nb * nc, 1, rows), f32),
                    pltpu.VMEM((blocks, 1, rows), f32),
                    pltpu.VMEM((blocks, 1, rows), f32),
                    pltpu.VMEM((1, feats), f32),
                    pltpu.VMEM((1, feats), f32),
                    pltpu.VMEM((blocks, 1, rows), f32),
                    dma,
                    dma((2 * nc,)),
                    dma((2 * nc,)),
                    dma((2 * nc,)),
                    dma((2 * nc,)),
                    dma((nc * ns,)),
                    dma((nc * ns,)),
                    dma((nb * nc,)),
                    dma((nb * nc,)),
                    dma,
                    dma,
                ],
                compiler_params=pltpu.CompilerParams(
                    collective_id=1 + number,
                    has_side_effects=True,
                    vmem_limit_bytes=62 * 2**20,
                ),
            )(x, counts, asked)

        return call

    which = sum((need[0, 0] > cap).astype(jnp.int32) for cap in caps[:-1])
    out = lax.switch(
        which,
        [with_cap(number, cap) for number, cap in enumerate(caps)],
        embeddings.reshape(blocks * bu, ur, feats),
        counts,
        asked,
    )
    return out.reshape(blocks, rows)


def solution(mesh):
    in_specs = (
        P(("groups", "clus", "sub"), None, None),
        P("groups"),
        P(None, ("groups", "clus", "sub", "rep"), None),
    )
    out_specs = P(("groups", "clus", "sub"), None)
    return jax.shard_map(
        on_device, mesh=mesh, in_specs=in_specs, out_specs=out_specs, check_vma=False
    )
```
